32 devices in a mesh: dp: 4 (over y, x), space: 8 (over z, core).
Axes of the slice: x: 2, y: 2, z: 4, core: 2. Of those that a mesh axis runs over, the one named last changes fastest.
Arguments:
- volumes: bfloat16 [4, 4, 32, 16, 256], P('dp', None, 'space'), may hold values from -6 to 6
- targets: float32 [4, 4], P('dp'), may hold values from -4 to 4
- first_kernel: bfloat16 [16, 4, 3, 3, 3], replicated, may hold values from -1 to 1
- first_bias: float32 [16], replicated, may hold values from -0.54 to -0.43
- second_kernel: bfloat16 [128, 16, 3, 3, 3], replicated, may hold values from -0.3125 to 0.3125
- second_bias: float32 [128], replicated, may hold values from -0.4 to 0.4
- head_weight: float32 [4, 128], replicated, may hold values from -0.5 to 0.5
- head_bias: float32 [4], replicated, may hold values from -3 to 3
Outputs:
- prediction: float32 [4, 4], P('dp')
- grad_first_kernel: float32 [16, 4, 3, 3, 3], replicated
- grad_first_bias: float32 [16], replicated
- grad_second_kernel: float32 [128, 16, 3, 3, 3], replicated
- grad_second_bias: float32 [128], replicated
- grad_head_weight: float32 [4, 128], replicated
- grad_head_bias: float32 [4], replicated
The draws below stay inside these ranges and needn't reach their ends.
All inputs are finite; a program needn't handle non-finite values.
Results may differ from the reference program's by a relative error of at most 0.0034.
Values may be sent and summed in bfloat16 or wider, within the bound.
A program may use at most 128 MiB of HBM per device.

```python
import jax
import jax.numpy as jnp
from jax import lax

CIN = 4
C1 = 16
C2 = 128
OUTS = 4
NY = 16
NZ = 256
NX = 32
SAMPLES = 4


def draw_volumes(key, part):
    own_key = jax.random.fold_in(key, 11)
    extent = (SAMPLES, CIN, NX, NY, NZ)
    values = jnp.clip(jax.random.normal(own_key, extent, jnp.float32), -6.0, 6.0)
    return values.astype(jnp.bfloat16)


def draw_first_kernel(key, part):
    own_key = jax.random.fold_in(key, 23)
    extent = (C1, CIN, 3, 3, 3)
    spread = (27.0 * CIN) ** (-0.5)
    values = jnp.clip(jax.random.normal(own_key, extent, jnp.float32), -5.0, 5.0) * spread
    return values.astype(jnp.bfloat16)


def block_scale(key, shape, shards, low, largest):
    def one(dim, shards_of):
        heights = jax.random.uniform(jax.random.fold_in(jax.random.fold_in(key, 6), dim), (shards_of,), jnp.float32, low / len(shards), largest / len(shards))
        return jnp.repeat(jnp.exp(heights), shape[dim] // shards_of).reshape((-1,) + (1,) * (len(shape) - dim - 1))

    gain = one(*shards[0])
    for cut in shards[1:]:
        gain = gain * one(*cut)
    return gain


def centred(rng, shape, scale, limit, split=(), dtype=jnp.bfloat16):
    array = jax.random.normal(rng, shape, jnp.float32) * scale
    if len(split) > 0:
        array = block_scale(rng, shape, split, -0.22, 0.18) * array
    return jnp.clip(array, min=-limit, max=limit).astype(dtype)


def setup_inputs(seed: int = 0) -> dict:
    streams_of = jax.random.split(jax.random.key(seed), 9)
    return {
        "volumes": draw_volumes(jax.random.fold_in(streams_of[8], 71), 0),
        "targets": centred(streams_of[1], (SAMPLES, OUTS), 1.0, 4.0, ((0, 4),), jnp.float32),
        "first_kernel": draw_first_kernel(jax.random.fold_in(streams_of[8], 71), 0),
        "first_bias": jnp.clip(jax.random.uniform(streams_of[3], (C1,), jnp.float32, -0.54, -0.43), -0.54, -0.43),
        "second_kernel": centred(streams_of[4], (C2, C1, 3, 3, 3), (27 * C1) ** -0.5, 0.3125),
        "second_bias": centred(streams_of[5], (C2,), 0.1, 0.4, (), jnp.float32),
        "head_weight": centred(streams_of[6], (OUTS, C2), C2 ** -0.5, 0.5, (), jnp.float32),
        "head_bias": centred(streams_of[7], (OUTS,), 1.0, 3.0, (), jnp.float32),
    }


def convolve(volume, kernel):
    return lax.conv_general_dilated(volume, kernel, (1, 1, 1), [(1, 1), (1, 1), (1, 1)], dimension_numbers=('NCDHW', 'OIDHW', 'NCDHW'), precision=lax.Precision.HIGHEST)

def leaky_slope(values):
    return jnp.where(values > 0, 1.0, 0.3).astype(jnp.float32)

def pool_cells(values):
    chans, size_x, size_y, size_z = values.shape
    blocks = values.reshape(chans, size_x // 2, 2, size_y // 2, 2, size_z // 2, 2)
    return lax.optimization_barrier(jnp.sum(blocks, axis=(2, 4, 6))) * 0.125

def spread_cells(values):
    chans, size_x, size_y, size_z = values.shape
    grown = jnp.broadcast_to(values[:, :, None, :, None, :, None], (chans, size_x, 2, size_y, 2, size_z, 2))
    return grown.reshape(chans, 2 * size_x, 2 * size_y, 2 * size_z)

def reference(volumes, targets, first_kernel, first_bias, second_kernel, second_bias, head_weight, head_bias):
    kernel_one = first_kernel.astype(jnp.float32)
    kernel_two = second_kernel.astype(jnp.float32)
    hp = lax.Precision.HIGHEST

    def one_sample(pair):
        volume, target_row = pair
        inputs = volume.astype(jnp.float32)[None]
        pre_first = convolve(inputs, kernel_one)[0] + first_bias[:, None, None, None]
        pooled = pool_cells(pre_first * leaky_slope(pre_first)).astype(jnp.bfloat16)
        pooled_f = pooled.astype(jnp.float32)[None]
        pre_second = convolve(pooled_f, kernel_two)[0] + second_bias[:, None, None, None]
        cells_two = pre_second.shape[1] * pre_second.shape[2] * pre_second.shape[3]
        features = lax.optimization_barrier(jnp.sum(pre_second * leaky_slope(pre_second), axis=(1, 2, 3))) / cells_two
        prediction = jnp.dot(head_weight, features, precision=hp) + head_bias
        grad_pred = 2.0 * (prediction - target_row) / SAMPLES
        grad_features = jnp.dot(head_weight.T, grad_pred, precision=hp)
        scaled = grad_features / cells_two
        grad_second = (scaled[:, None, None, None] * leaky_slope(pre_second)).astype(jnp.bfloat16)
        second_f = grad_second.astype(jnp.float32)[None]
        _, pull_kernel_two = jax.vjp(lambda kern: convolve(pooled_f, kern), kernel_two)
        grad_kernel_two = pull_kernel_two(second_f)[0]
        _, pull_input_two = jax.vjp(lambda vol: convolve(vol, kernel_two), pooled_f)
        grad_pooled = pull_input_two(second_f)[0][0]
        grad_first = (spread_cells(grad_pooled * 0.125) * leaky_slope(pre_first)).astype(jnp.bfloat16)
        first_f = grad_first.astype(jnp.float32)[None]
        _, pull_kernel_one = jax.vjp(lambda kern: convolve(inputs, kern), kernel_one)
        grad_kernel_one = pull_kernel_one(first_f)[0]
        return (prediction, grad_kernel_one, lax.optimization_barrier(jnp.sum(first_f, axis=(0, 2, 3, 4))), grad_kernel_two, lax.optimization_barrier(jnp.sum(second_f, axis=(0, 2, 3, 4))), grad_pred[:, None] * features[None, :], grad_pred)
    results = lax.map(one_sample, (volumes, targets))
    return (results[0], lax.optimization_barrier(jnp.sum(results[1], axis=0)), lax.optimization_barrier(jnp.sum(results[2], axis=0)), lax.optimization_barrier(jnp.sum(results[3], axis=0)), lax.optimization_barrier(jnp.sum(results[4], axis=0)), lax.optimization_barrier(jnp.sum(results[5], axis=0)), lax.optimization_barrier(jnp.sum(results[6], axis=0)))
```

```python
import functools

import jax
import jax.numpy as jnp
from jax import lax
from jax.experimental import pallas as pl
from jax.experimental.pallas import tpu as pltpu
from jax.sharding import PartitionSpec as P

F32 = jnp.float32
BF16 = jnp.bfloat16
MESH = pl.DeviceIdType.MESH
NT = (((1,), (1,)), ((), ()))
TN = (((0,), (0,)), ((), ()))
EARLY = 448
ROWS = 624


def iota(shape, dim):
    return lax.broadcasted_iota(jnp.int32, shape, dim)


def dot(a, b, dims=(((1,), (0,)), ((), ())), precision=None):
    return lax.dot_general(a, b, dims, precision=precision, preferred_element_type=F32)


def to_column(row):
    n = row.shape[1]
    return jnp.sum(jnp.where(iota((n, n), 0) == iota((n, n), 1), row, 0.0), axis=1, keepdims=True)


def to_row(column):
    n = column.shape[0]
    return jnp.sum(jnp.where(iota((n, n), 0) == iota((n, n), 1), column, 0.0), axis=0, keepdims=True)


def shifted(block, dz):
    if dz == 1:
        return block
    lane = iota(block.shape, 1)
    if dz == 0:
        return jnp.where(lane == 0, 0.0, pltpu.roll(block, 1, 1))
    return jnp.where(lane == 127, 0.0, pltpu.roll(block, 127, 1))


def kernel(
    n, nd,
    vol, tgt, k1m, b1, k2t, b2, hw, hb,
    pred_o, gk1_o, gb1_o, gk2_o, gb2_o, gh_o, ghb_o,
    lo1, hi1, lo2, hi2, patch, patch3, w1, own1, pz, p2, mk, mo, zs, ga, gg, acc1,
    fbuf, buf, rsbuf, dpbuf, res,
    h_send, h_recv, f_send, f_recv, r_send, r_recv, d_send, d_recv, g_send, g_recv,
):
    me = lax.axis_index("space")
    md = lax.axis_index("dp")
    samples = nd
    cells_two = 2 * 8 * 128 * n
    shard = buf.shape[0] // n

    def peer(j):
        return lax.rem(me + j, n)

    def dpeer(j):
        return lax.rem(md + j, nd)

    barrier = pltpu.get_barrier_semaphore()
    for j in range(1, n):
        pl.semaphore_signal(barrier, inc=1, device_id={"space": peer(j)}, device_id_type=MESH)
    for j in range(1, nd):
        pl.semaphore_signal(barrier, inc=1, device_id={"dp": dpeer(j)}, device_id_type=MESH)

    def remote(src, dst, send, recv, axis, to):
        return pltpu.make_async_remote_copy(
            src_ref=src, dst_ref=dst, send_sem=send, recv_sem=recv,
            device_id={axis: to}, device_id_type=MESH,
        )

    split = (iota((256, 512), 0) == 2 * (iota((256, 512), 1) & 127) + (iota((256, 512), 1) >> 7) - 1)
    split = split.astype(F32).astype(BF16)

    def place(blocks, first):
        rows = jnp.concatenate([blk.reshape(64, 256) for blk in blocks], axis=0)
        parts = dot(rows, split).astype(BF16)
        for i in range(len(blocks)):
            for s in range(4):
                patch[s * 64:(s + 1) * 64, (first + i) * 128:(first + i + 1) * 128] = (
                    parts[i * 64:(i + 1) * 64, s * 128:(s + 1) * 128]
                )

    pl.semaphore_wait(barrier, n - 1 + nd - 1)

    first = [vol, vol, vol.at[:, 3:4], vol.at[:, 0:1]]
    into = [lo1, hi1, lo2, hi2]
    steps = [1, -1, 2, -2]
    halo = [
        remote(first[i], into[i], h_send.at[i], h_recv.at[i], "space", lax.rem(me + steps[i] + n, n))
        for i in range(4)
    ]
    has_to = [me < n - 1, me > 0, me < n - 2, me > 1]
    has_from = [me > 0, me < n - 1, me > 1, me < n - 2]
    for i in range(4):
        pl.when(has_to[i])(halo[i].start)
    for i in range(4):
        @pl.when(jnp.logical_not(has_from[i]))
        def _(i=i):
            into[i][...] = jnp.zeros_like(into[i])

    place([vol[:, x] for x in range(4)], 5)

    col = iota((12, 512), 1)
    tap = iota((12, 512), 0)
    pick = (((col & 63) >> 4) == (tap & 3)) & (((col & 255) >> 6) == (col >> 8) + (tap >> 2))
    spread = dot(k1m[...], pick.astype(F32).astype(BF16))
    ycol = iota((16, 256), 1) & 15
    for dx in range(3):
        for p in range(2):
            e = [spread[(dx * 3 + dy) * 16:(dx * 3 + dy + 1) * 16, p * 256:(p + 1) * 256] for dy in range(3)]
            for q in range(2):
                for yh in range(8):
                    y = 2 * yh + q
                    block = jnp.where(
                        ycol == y - 1, e[0],
                        jnp.where(ycol == y, e[1], jnp.where(ycol == y + 1, e[2], 0.0)),
                    )
                    r = p * 256 + (q * 8 + yh) * 16
                    w1[r:r + 16, dx * 256:(dx + 1) * 256] = block.astype(BF16)
    bias1 = jnp.broadcast_to(to_column(b1[...]), (16, 128))
    bias1 = jnp.concatenate([bias1] * 8, axis=0)
    bias2 = jnp.broadcast_to(to_column(b2[...]), (128, 128))

    pz[:, 0:16, :] = jnp.zeros((3, 16, 768), BF16)
    pz[:, 144:160, :] = jnp.zeros((3, 16, 768), BF16)
    p2[432:448, :] = jnp.ones((16, 4096), BF16)
    own = ((iota((128, 512), 1) >= 128) & (iota((128, 512), 1) < 384)).astype(F32)
    for y in range(8):
        mo[128:256, y * 512:(y + 1) * 512] = own.astype(BF16)
    buf[ROWS - 16:, :] = jnp.zeros((buf.shape[0] - ROWS + 16, 128), F32)

    for i in range(4):
        pl.when(has_from[i])(halo[i].wait_recv)
    place([lo2[:, 0]] + [lo1[:, x] for x in range(4)], 0)
    place([hi1[:, x] for x in range(4)] + [hi2[:, 0]], 9)
    for dx in range(3):
        patch3[dx * 256:(dx + 1) * 256, :] = patch[:, dx * 128:dx * 128 + 1536]

    low_ok = jnp.where(me > 0, 1.0, 0.0).astype(F32)
    high_ok = jnp.where(me < n - 1, 1.0, 0.0).astype(F32)
    for xp in range(6):
        pre = dot(w1[...], patch3[:, xp * 256:(xp + 1) * 256])
        total = None
        for r in range(4):
            for x in range(2):
                part = pre[r * 128:(r + 1) * 128, x * 128:(x + 1) * 128] + bias1
                if 2 <= xp < 4:
                    c = (xp - 2) * 256 + x * 128
                    own1[r * 128:(r + 1) * 128, c:c + 128] = part
                part = jnp.where(part > 0, part, 0.3 * part)
                total = part if total is None else total + part
        total = total * 0.125
        if xp < 2:
            total = total * low_ok
        if xp > 3:
            total = total * high_ok
        for dz in range(3):
            pz[dz, 16:144, xp * 128:(xp + 1) * 128] = shifted(total, dz).astype(BF16)

    for dx in range(3):
        for dy in range(3):
            for dz in range(3):
                t = (dx * 3 + dy) * 3 + dz
                for y in range(8):
                    p2[t * 16:(t + 1) * 16, y * 512:(y + 1) * 512] = (
                        pz[dz, (y + dy) * 16:(y + dy + 1) * 16, dx * 128:dx * 128 + 512]
                    )

    fsum = jnp.zeros((128, 128), F32)
    for y in range(8):
        pre = dot(k2t[...], p2[0:432, y * 512:(y + 1) * 512], TN)
        for x in range(4):
            lanes = slice(y * 512 + x * 128, y * 512 + (x + 1) * 128)
            part = pre[:, x * 128:(x + 1) * 128] + bias2
            mask = jnp.where(part > 0, 1.0, 0.0)
            mk[:, lanes] = mask.astype(BF16)
            if 1 <= x < 3:
                fsum = fsum + jnp.where(part > 0, part, 0.3 * part)
                mo[0:128, lanes] = mask.astype(BF16)
            else:
                mo[0:128, lanes] = jnp.zeros((128, 128), BF16)

    frow = jnp.sum(fsum.T, axis=0, keepdims=True)
    fbuf[me] = jnp.broadcast_to(frow, (8, 128))
    feats = [
        remote(fbuf.at[me], fbuf.at[me], f_send.at[j], f_recv.at[me], "space", peer(j))
        for j in range(1, n)
    ]
    for copy in feats:
        copy.start()

    sums = dot(p2[...], mo[...], NT)

    def arrived(slots, sems, axis, source):
        remote(slots.at[source], slots.at[source], f_send.at[0], sems.at[source], axis, source).wait_recv()

    for j in range(1, n):
        arrived(fbuf, f_recv, "space", peer(j))
    total = fbuf[0]
    for s in range(1, n):
        total = total + fbuf[s]
    features = total[0:4] / cells_two
    head = hw[...]
    prediction = jnp.sum(head * features, axis=1, keepdims=True) + to_column(hb[...])
    grad_pred = 2.0 * (prediction - to_column(tgt[...])) / samples
    pred_o[...] = to_row(prediction)
    scaled = jnp.sum(head * grad_pred, axis=0, keepdims=True) / cells_two
    plus = scaled.astype(BF16).astype(F32)
    minus = (0.3 * scaled).astype(BF16).astype(F32)
    leader = jnp.where(me == 0, 1.0, 0.0).astype(F32)

    buf[0:EARLY, :] = sums[:, 128:256] * minus + sums[:, 0:128] * (plus - minus)
    buf[608:612, :] = leader * (grad_pred * features)
    buf[616:620, :] = leader * jnp.broadcast_to(grad_pred, (4, 128))

    whole = EARLY // shard
    scatter = [
        remote(
            buf.at[pl.ds(pl.multiple_of(peer(j) * shard, 8), shard)], rsbuf.at[me],
            r_send.at[j], r_recv.at[me], "space", peer(j),
        )
        for j in range(1, n)
    ]
    for j in range(1, n):
        pl.when(peer(j) < whole)(scatter[j - 1].start)

    plus_c = jnp.broadcast_to(plus, (128, 128)).T
    minus_c = jnp.broadcast_to(minus, (128, 128)).T
    for y in range(8):
        parts = []
        for x in range(4):
            part = mk[:, y * 512 + x * 128:y * 512 + (x + 1) * 128].astype(F32)
            part = jnp.where(part > 0, plus_c, minus_c)
            if x == 0:
                part = part * low_ok
            if x == 3:
                part = part * high_ok
            parts.append(part.astype(BF16))
        zs[:, y * 512:(y + 1) * 512] = dot(k2t[...], jnp.concatenate(parts, axis=1))
    for y in range(8):
        for dz in range(3):
            total = None
            for dx in range(3):
                for dy in range(3):
                    ys = y + 1 - dy
                    if 0 <= ys < 8:
                        t = (dx * 3 + dy) * 3 + dz
                        c = ys * 512 + (2 - dx) * 128
                        part = zs[t * 16:(t + 1) * 16, c:c + 256]
                        total = part if total is None else total + part
            ga[dz, y * 16:(y + 1) * 16, :] = total
    bsum = jnp.zeros((16, 128), F32)
    for xp in range(2):
        lanes = slice(xp * 128, (xp + 1) * 128)
        g = shifted(ga[0, :, lanes], 2) + ga[1, :, lanes] + shifted(ga[2, :, lanes], 0)
        g = g * 0.125
        low = 0.3 * g
        for r in range(4):
            for x in range(2):
                c = xp * 256 + x * 128
                part = jnp.where(own1[r * 128:(r + 1) * 128, c:c + 128] > 0, g, low).astype(BF16)
                gg[r * 128:(r + 1) * 128, c:c + 128] = part
                part = part.astype(F32)
                for k in range(8):
                    bsum = bsum + part[k * 16:(k + 1) * 16]
    for dx in range(3):
        full = dot(gg[...], patch3[dx * 256:(dx + 1) * 256, 512:1024], NT)
        for p in range(2):
            accs = [jnp.zeros((16, 256), F32)] * 3
            for q in range(2):
                for yh in range(8):
                    y = 2 * yh + q
                    r = p * 256 + (q * 8 + yh) * 16
                    block = full[r:r + 16, :]
                    for dy in range(3):
                        accs[dy] = accs[dy] + jnp.where(ycol == y + dy - 1, block, 0.0)
            for dy in range(3):
                r = (dx * 3 + dy) * 16
                acc1[r:r + 16, p * 256:(p + 1) * 256] = accs[dy]
    col = iota((128, 512), 1)
    tap = iota((128, 512), 0)
    pick = (((col & 63) >> 4) == (tap & 3)) & (((col & 255) >> 6) == (col >> 8) + (tap >> 2)) & (tap < 12)
    buf[448:592, :] = dot(acc1[...], pick.astype(F32), NT, lax.Precision.HIGHEST)
    buf[592:608, :] = bsum
    for j in range(1, n):
        pl.when(peer(j) >= whole)(scatter[j - 1].start)

    for j in range(1, n):
        arrived(rsbuf, r_recv, "space", peer(j))
    rsbuf[me] = buf[pl.ds(pl.multiple_of(me * shard, 8), shard), :]
    total = rsbuf[0]
    for s in range(1, n):
        total = total + rsbuf[s]
    dpbuf[md] = total
    across = [
        remote(dpbuf.at[md], dpbuf.at[md], d_send.at[j], d_recv.at[md], "dp", dpeer(j))
        for j in range(1, nd)
    ]
    for copy in across:
        copy.start()
    for j in range(1, nd):
        arrived(dpbuf, d_recv, "dp", dpeer(j))
    total = dpbuf[0]
    for s in range(1, nd):
        total = total + dpbuf[s]
    mine = pl.ds(pl.multiple_of(me * shard, 8), shard)
    res[mine, :] = total
    gather = [
        remote(res.at[mine], res.at[mine], g_send.at[j], g_recv.at[me], "space", peer(j))
        for j in range(1, n)
    ]
    for copy in gather:
        copy.start()
    for j in range(1, n):
        source = peer(j)
        part = res.at[pl.ds(pl.multiple_of(source * shard, 8), shard)]
        remote(part, part, f_send.at[0], g_recv.at[source], "space", source).wait_recv()

    gk2_o[...] = res[0:432, :]
    gb2_o[...] = res[432:433, :]
    gk1_o[...] = res[448:592, 0:12]
    gb1_o[...] = to_row(jnp.sum(res[592:608, :], axis=1, keepdims=True))
    gh_o[...] = res[608:612, :]
    ghb_o[...] = to_row(res[616:620, 0:1])

    for i in range(4):
        pl.when(has_to[i])(halo[i].wait_send)
    for copy in feats + scatter + across + gather:
        copy.wait_send()


def body(
    volumes, targets, first_kernel, first_bias, second_kernel, second_bias, head_weight, head_bias
):
    n = lax.axis_size("space")
    nd = lax.axis_size("dp")
    shard = -(-ROWS // (8 * n)) * 8
    k1m = first_kernel.transpose(2, 3, 0, 4, 1).reshape(144, 12)
    k2t = second_kernel.transpose(2, 3, 4, 1, 0).reshape(432, 128)
    shape = jax.ShapeDtypeStruct
    sem = pltpu.SemaphoreType.DMA
    v = pltpu.VMEM
    pred, gk1, gb1, gk2, gb2, gh, ghb = pl.pallas_call(
        functools.partial(kernel, n, nd),
        out_shape=(
            shape((1, 4), F32), shape((144, 12), F32), shape((1, 16), F32), shape((432, 128), F32),
            shape((1, 128), F32), shape((4, 128), F32), shape((1, 4), F32),
        ),
        in_specs=[pl.BlockSpec(memory_space=pltpu.VMEM)] * 8,
        out_specs=[pl.BlockSpec(memory_space=pltpu.VMEM)] * 7,
        scratch_shapes=[
            v((4, 4, 16, 256), BF16), v((4, 4, 16, 256), BF16),
            v((4, 1, 16, 256), BF16), v((4, 1, 16, 256), BF16),
            v((256, 1792), BF16), v((768, 1536), BF16), v((512, 768), BF16), v((512, 512), F32),
            v((3, 160, 768), BF16), v((448, 4096), BF16), v((128, 4096), BF16), v((256, 4096), BF16),
            v((432, 4096), F32), v((3, 128, 256), F32), v((512, 512), BF16), v((144, 512), F32),
            v((n, 8, 128), F32), v((n * shard, 128), F32), v((n, shard, 128), F32),
            v((nd, shard, 128), F32), v((n * shard, 128), F32),
            sem((4,)), sem((4,)), sem((n,)), sem((n,)), sem((n,)), sem((n,)),
            sem((nd,)), sem((nd,)), sem((n,)), sem((n,)),
        ],
        compiler_params=pltpu.CompilerParams(
            collective_id=0, has_side_effects=True, vmem_limit_bytes=56 * 1024 * 1024
        ),
        cost_estimate=pl.CostEstimate(flops=5_000_000_000, bytes_accessed=2_000_000, transcendentals=0),
    )(
        volumes[0], targets, k1m, first_bias[None], k2t, second_bias[None], head_weight, head_bias[None]
    )
    gk1 = gk1.reshape(3, 3, 16, 3, 4).transpose(2, 4, 0, 1, 3)
    gk2 = gk2.reshape(3, 3, 3, 16, 128).transpose(4, 3, 0, 1, 2)
    return pred, gk1, gb1[0], gk2, gb2[0], gh, ghb[0]


def solution(mesh):
    in_specs = (P("dp", None, "space", None, None), P("dp", None), P(), P(), P(), P(), P(), P())
    out_specs = (P("dp", None), P(), P(), P(), P(), P(), P())
    return jax.shard_map(body, mesh=mesh, in_specs=in_specs, out_specs=out_specs, check_vma=False)
```

```python
import functools

import jax
import jax.numpy as jnp
from jax import lax
from jax.experimental import pallas as pl
from jax.experimental.pallas import tpu as pltpu
from jax.sharding import PartitionSpec as P

F32 = jnp.float32
BF16 = jnp.bfloat16
MESH = pl.DeviceIdType.MESH
NT = (((1,), (1,)), ((), ()))
TN = (((0,), (0,)), ((), ()))
EARLY = 448
ROWS = 512


def iota(shape, dim):
    return lax.broadcasted_iota(jnp.int32, shape, dim)


def dot(a, b, dims=(((1,), (0,)), ((), ())), precision=None):
    return lax.dot_general(a, b, dims, precision=precision, preferred_element_type=F32)


def to_column(row):
    n = row.shape[1]
    return jnp.sum(jnp.where(iota((n, n), 0) == iota((n, n), 1), row, 0.0), axis=1, keepdims=True)


def to_row(column):
    n = column.shape[0]
    return jnp.sum(jnp.where(iota((n, n), 0) == iota((n, n), 1), column, 0.0), axis=0, keepdims=True)


def shifted(block, dz):
    if dz == 1:
        return block
    lane = iota(block.shape, 1)
    if dz == 0:
        return jnp.where(lane == 0, 0.0, pltpu.roll(block, 1, 1))
    return jnp.where(lane == 127, 0.0, pltpu.roll(block, 127, 1))


def kernel(
    n, nd,
    vol, tgt, k1, b1, k2t, b2, hw, hb,
    res, pred_o,
    k1s, lo1, hi1, lo2, hi2, patch, patch3, w1, own1, pz, p2, mk, mo, zs, ga, gg, acc1,
    fbuf, buf, rsbuf, dpbuf,
    h_send, h_recv, f_send, f_recv, r_send, r_recv, d_send, d_recv, g_send, g_recv,
):
    me = lax.axis_index("space")
    md = lax.axis_index("dp")
    samples = nd
    cells_two = 2 * 8 * 128 * n
    shard = buf.shape[0] // n

    def peer(j):
        return lax.rem(me + j, n)

    def dpeer(j):
        return lax.rem(md + j, nd)

    barrier = pltpu.get_barrier_semaphore()
    for j in range(1, n):
        pl.semaphore_signal(barrier, inc=1, device_id={"space": peer(j)}, device_id_type=MESH)
    for j in range(1, nd):
        pl.semaphore_signal(barrier, inc=1, device_id={"dp": dpeer(j)}, device_id_type=MESH)

    def remote(src, dst, send, recv, axis, to):
        return pltpu.make_async_remote_copy(
            src_ref=src, dst_ref=dst, send_sem=send, recv_sem=recv,
            device_id={axis: to}, device_id_type=MESH,
        )

    split = (iota((256, 512), 0) == 2 * (iota((256, 512), 1) & 127) + (iota((256, 512), 1) >> 7) - 1)
    split = split.astype(F32).astype(BF16)

    def place(blocks, first):
        rows = jnp.concatenate([blk.reshape(64, 256) for blk in blocks], axis=0)
        parts = dot(rows, split).astype(BF16)
        for i in range(len(blocks)):
            for s in range(4):
                patch[s * 64:(s + 1) * 64, (first + i) * 128:(first + i + 1) * 128] = (
                    parts[i * 64:(i + 1) * 64, s * 128:(s + 1) * 128]
                )

    pl.semaphore_wait(barrier, n - 1 + nd - 1)

    first = [vol, vol, vol.at[:, 3:4], vol.at[:, 0:1]]
    into = [lo1, hi1, lo2, hi2]
    steps = [1, -1, 2, -2]
    halo = [
        remote(first[i], into[i], h_send.at[i], h_recv.at[i], "space", lax.rem(me + steps[i] + n, n))
        for i in range(4)
    ]
    has_to = [me < n - 1, me > 0, me < n - 2, me > 1]
    has_from = [me > 0, me < n - 1, me > 1, me < n - 2]
    for i in range(4):
        pl.when(has_to[i])(halo[i].start)
    for i in range(4):
        @pl.when(jnp.logical_not(has_from[i]))
        def _(i=i):
            into[i][...] = jnp.zeros_like(into[i])

    place([vol[:, x] for x in range(4)], 5)

    col = iota((12, 512), 1)
    tap = iota((12, 512), 0)
    pick = (((col & 63) >> 4) == (tap & 3)) & (((col & 255) >> 6) == (col >> 8) + (tap >> 2))
    for t in range(9):
        for dz in range(3):
            k1s[dz * 4:(dz + 1) * 4, t * 16:(t + 1) * 16] = k1[t * 3 + dz].astype(F32)
    spread = dot(k1s[0:12, 0:144].astype(BF16), pick.astype(F32).astype(BF16), TN)
    ycol = iota((16, 256), 1) & 15
    for dx in range(3):
        for p in range(2):
            e = [spread[(dx * 3 + dy) * 16:(dx * 3 + dy + 1) * 16, p * 256:(p + 1) * 256] for dy in range(3)]
            for q in range(2):
                for yh in range(8):
                    y = 2 * yh + q
                    block = jnp.where(
                        ycol == y - 1, e[0],
                        jnp.where(ycol == y, e[1], jnp.where(ycol == y + 1, e[2], 0.0)),
                    )
                    r = p * 256 + (q * 8 + yh) * 16
                    w1[r:r + 16, dx * 256:(dx + 1) * 256] = block.astype(BF16)
    bias1 = jnp.broadcast_to(to_column(b1[...]), (16, 128))
    bias1 = jnp.concatenate([bias1] * 8, axis=0)
    bias2 = jnp.broadcast_to(to_column(b2[...]), (128, 128))

    pz[:, 0:16, :] = jnp.zeros((3, 16, 768), BF16)
    pz[:, 144:160, :] = jnp.zeros((3, 16, 768), BF16)
    p2[432:448, :] = jnp.ones((16, 4096), BF16)
    own = ((iota((128, 512), 1) >= 128) & (iota((128, 512), 1) < 384)).astype(F32)
    for y in range(8):
        mo[128:256, y * 512:(y + 1) * 512] = own.astype(BF16)
    buf[EARLY:, :] = jnp.zeros((buf.shape[0] - EARLY, 128), F32)

    for i in range(4):
        pl.when(has_from[i])(halo[i].wait_recv)
    place([lo2[:, 0]] + [lo1[:, x] for x in range(4)], 0)
    place([hi1[:, x] for x in range(4)] + [hi2[:, 0]], 9)
    for dx in range(3):
        patch3[dx * 256:(dx + 1) * 256, :] = patch[:, dx * 128:dx * 128 + 1536]

    low_ok = jnp.where(me > 0, 1.0, 0.0).astype(F32)
    high_ok = jnp.where(me < n - 1, 1.0, 0.0).astype(F32)
    for xp in range(6):
        pre = dot(w1[...], patch3[:, xp * 256:(xp + 1) * 256])
        total = None
        for r in range(4):
            for x in range(2):
                part = pre[r * 128:(r + 1) * 128, x * 128:(x + 1) * 128] + bias1
                if 2 <= xp < 4:
                    c = (xp - 2) * 256 + x * 128
                    own1[r * 128:(r + 1) * 128, c:c + 128] = part
                part = jnp.where(part > 0, part, 0.3 * part)
                total = part if total is None else total + part
        total = total * 0.125
        if xp < 2:
            total = total * low_ok
        if xp > 3:
            total = total * high_ok
        for dz in range(3):
            pz[dz, 16:144, xp * 128:(xp + 1) * 128] = shifted(total, dz).astype(BF16)

    for dx in range(3):
        for dy in range(3):
            for dz in range(3):
                t = (dx * 3 + dy) * 3 + dz
                for y in range(8):
                    p2[t * 16:(t + 1) * 16, y * 512:(y + 1) * 512] = (
                        pz[dz, (y + dy) * 16:(y + dy + 1) * 16, dx * 128:dx * 128 + 512]
                    )

    fsum = jnp.zeros((128, 128), F32)
    for y in range(8):
        pre = dot(k2t[...], p2[0:432, y * 512:(y + 1) * 512], TN)
        for x in range(4):
            lanes = slice(y * 512 + x * 128, y * 512 + (x + 1) * 128)
            part = pre[:, x * 128:(x + 1) * 128] + bias2
            mask = jnp.where(part > 0, 1.0, 0.0)
            mk[:, lanes] = mask.astype(BF16)
            if 1 <= x < 3:
                fsum = fsum + jnp.where(part > 0, part, 0.3 * part)
                mo[0:128, lanes] = mask.astype(BF16)
            else:
                mo[0:128, lanes] = jnp.zeros((128, 128), BF16)

    frow = jnp.sum(fsum.T, axis=0, keepdims=True)
    fbuf[me] = jnp.broadcast_to(frow, (8, 128))
    feats = [
        remote(fbuf.at[me], fbuf.at[me], f_send.at[j], f_recv.at[me], "space", peer(j))
        for j in range(1, n)
    ]
    for copy in feats:
        copy.start()

    sums = dot(p2[...], mo[...], NT)

    def arrived(slots, sems, axis, source):
        remote(slots.at[source], slots.at[source], f_send.at[0], sems.at[source], axis, source).wait_recv()

    for j in range(1, n):
        arrived(fbuf, f_recv, "space", peer(j))
    total = fbuf[0]
    for s in range(1, n):
        total = total + fbuf[s]
    features = total[0:4] / cells_two
    head = hw[...]
    prediction = jnp.sum(head * features, axis=1, keepdims=True) + to_column(hb[...])
    grad_pred = 2.0 * (prediction - to_column(tgt[...])) / samples
    pred_o[...] = jnp.broadcast_to(prediction, (4, 128))
    scaled = jnp.sum(head * grad_pred, axis=0, keepdims=True) / cells_two
    plus = scaled.astype(BF16).astype(F32)
    minus = (0.3 * scaled).astype(BF16).astype(F32)
    leader = jnp.where(me == 0, 1.0, 0.0).astype(F32)

    buf[0:EARLY, :] = sums[:, 128:256] * minus + sums[:, 0:128] * (plus - minus)
    buf[496:500, :] = leader * (grad_pred * features)
    buf[504:508, :] = leader * jnp.broadcast_to(grad_pred, (4, 128))

    whole = EARLY // shard
    scatter = [
        remote(
            buf.at[pl.ds(pl.multiple_of(peer(j) * shard, 8), shard)], rsbuf.at[me],
            r_send.at[j], r_recv.at[me], "space", peer(j),
        )
        for j in range(1, n)
    ]
    for j in range(1, n):
        pl.when(peer(j) < whole)(scatter[j - 1].start)

    plus_c = jnp.broadcast_to(plus, (128, 128)).T
    minus_c = jnp.broadcast_to(minus, (128, 128)).T
    for y in range(8):
        parts = []
        for x in range(4):
            part = mk[:, y * 512 + x * 128:y * 512 + (x + 1) * 128].astype(F32)
            part = jnp.where(part > 0, plus_c, minus_c)
            if x == 0:
                part = part * low_ok
            if x == 3:
                part = part * high_ok
            parts.append(part.astype(BF16))
        zs[:, y * 512:(y + 1) * 512] = dot(k2t[...], jnp.concatenate(parts, axis=1))
    for y in range(8):
        for dz in range(3):
            total = None
            for dx in range(3):
                for dy in range(3):
                    ys = y + 1 - dy
                    if 0 <= ys < 8:
                        t = (dx * 3 + dy) * 3 + dz
                        c = ys * 512 + (2 - dx) * 128
                        part = zs[t * 16:(t + 1) * 16, c:c + 256]
                        total = part if total is None else total + part
            ga[dz, y * 16:(y + 1) * 16, :] = total
    bsum = jnp.zeros((16, 128), F32)
    for xp in range(2):
        lanes = slice(xp * 128, (xp + 1) * 128)
        g = shifted(ga[0, :, lanes], 2) + ga[1, :, lanes] + shifted(ga[2, :, lanes], 0)
        g = g * 0.125
        low = 0.3 * g
        for r in range(4):
            for x in range(2):
                c = xp * 256 + x * 128
                part = jnp.where(own1[r * 128:(r + 1) * 128, c:c + 128] > 0, g, low).astype(BF16)
                gg[r * 128:(r + 1) * 128, c:c + 128] = part
                part = part.astype(F32)
                for k in range(8):
                    bsum = bsum + part[k * 16:(k + 1) * 16]
    for dx in range(3):
        full = dot(gg[...], patch3[dx * 256:(dx + 1) * 256, 512:1024], NT)
        for p in range(2):
            accs = [jnp.zeros((16, 256), F32)] * 3
            for q in range(2):
                for yh in range(8):
                    y = 2 * yh + q
                    r = p * 256 + (q * 8 + yh) * 16
                    block = full[r:r + 16, :]
                    for dy in range(3):
                        accs[dy] = accs[dy] + jnp.where(ycol == y + dy - 1, block, 0.0)
            for dy in range(3):
                r = (dx * 3 + dy) * 16
                acc1[r:r + 16, p * 256:(p + 1) * 256] = accs[dy]
    col = iota((16, 512), 1)
    tap = iota((16, 512), 0)
    pick = (((col & 63) >> 4) == (tap & 3)) & (((col & 255) >> 6) == (col >> 8) + (tap >> 2)) & (tap < 12)
    first = dot(pick.astype(F32), acc1[...], NT, lax.Precision.HIGHEST)
    buf[448:464, :] = first[:, 0:128]
    buf[464:480, 0:16] = first[:, 128:144]
    buf[480:496, :] = jnp.broadcast_to(jnp.sum(bsum, axis=1, keepdims=True), (16, 128))
    for j in range(1, n):
        pl.when(peer(j) >= whole)(scatter[j - 1].start)

    for j in range(1, n):
        arrived(rsbuf, r_recv, "space", peer(j))
    rsbuf[me] = buf[pl.ds(pl.multiple_of(me * shard, 8), shard), :]
    total = rsbuf[0]
    for s in range(1, n):
        total = total + rsbuf[s]
    dpbuf[md] = total
    across = [
        remote(dpbuf.at[md], dpbuf.at[md], d_send.at[j], d_recv.at[md], "dp", dpeer(j))
        for j in range(1, nd)
    ]
    for copy in across:
        copy.start()
    for j in range(1, nd):
        arrived(dpbuf, d_recv, "dp", dpeer(j))
    total = dpbuf[0]
    for s in range(1, nd):
        total = total + dpbuf[s]
    mine = pl.ds(pl.multiple_of(me * shard, 16), shard)
    res[mine, :] = total.astype(BF16)
    gather = [
        remote(res.at[mine], res.at[mine], g_send.at[j], g_recv.at[me], "space", peer(j))
        for j in range(1, n)
    ]
    for copy in gather:
        copy.start()
    for j in range(1, n):
        source = peer(j)
        part = res.at[pl.ds(pl.multiple_of(source * shard, 16), shard)]
        remote(part, part, f_send.at[0], g_recv.at[source], "space", source).wait_recv()

    for i in range(4):
        pl.when(has_to[i])(halo[i].wait_send)
    for copy in feats + scatter + across + gather:
        copy.wait_send()


def finish(res, pred, pred_o, gk1_o, gb1_o, gk2_o, gb2_o, gh_o, ghb_o):
    gk2_o[...] = res[0:432, :].astype(F32)
    rest = res[432:512, :].astype(F32)
    gb2_o[...] = rest[0:1]
    for t in range(9):
        r, c = (16, t * 16) if t < 8 else (32, 0)
        for dz in range(3):
            gk1_o[t * 3 + dz] = rest[r + dz * 4:r + (dz + 1) * 4, c:c + 16]
    gb1_o[...] = to_row(rest[48:64, 0:1])
    gh_o[...] = rest[64:68]
    ghb_o[...] = to_row(rest[72:76, 0:1])
    pred_o[...] = to_row(pred[:, 0:1])


def body(
    volumes, targets, first_kernel, first_bias, second_kernel, second_bias, head_weight, head_bias
):
    n = lax.axis_size("space")
    nd = lax.axis_size("dp")
    shard = -(-ROWS // (16 * n)) * 16
    k1 = first_kernel.transpose(2, 3, 4, 1, 0).reshape(27, 4, 16)
    k2t = second_kernel.transpose(2, 3, 4, 1, 0).reshape(432, 128)
    shape = jax.ShapeDtypeStruct
    sem = pltpu.SemaphoreType.DMA
    v = pltpu.VMEM
    res, pred = pl.pallas_call(
        functools.partial(kernel, n, nd),
        out_shape=(shape((n * shard, 128), BF16), shape((4, 128), F32)),
        in_specs=[pl.BlockSpec(memory_space=pltpu.VMEM)] * 8,
        out_specs=[pl.BlockSpec(memory_space=pltpu.VMEM)] * 2,
        scratch_shapes=[
            v((16, 256), F32),
            v((4, 4, 16, 256), BF16), v((4, 4, 16, 256), BF16),
            v((4, 1, 16, 256), BF16), v((4, 1, 16, 256), BF16),
            v((256, 1792), BF16), v((768, 1536), BF16), v((512, 768), BF16), v((512, 512), F32),
            v((3, 160, 768), BF16), v((448, 4096), BF16), v((128, 4096), BF16), v((256, 4096), BF16),
            v((432, 4096), F32), v((3, 128, 256), F32), v((512, 512), BF16), v((144, 512), F32),
            v((n, 8, 128), F32), v((n * shard, 128), F32), v((n, shard, 128), F32),
            v((nd, shard, 128), F32),
            sem((4,)), sem((4,)), sem((n,)), sem((n,)), sem((n,)), sem((n,)),
            sem((nd,)), sem((nd,)), sem((n,)), sem((n,)),
        ],
        compiler_params=pltpu.CompilerParams(
            collective_id=0, has_side_effects=True, vmem_limit_bytes=56 * 1024 * 1024
        ),
        cost_estimate=pl.CostEstimate(flops=5_000_000_000, bytes_accessed=2_000_000, transcendentals=0),
    )(
        volumes[0], targets, k1, first_bias[None], k2t, second_bias[None], head_weight, head_bias[None]
    )
    pred, gk1, gb1, gk2, gb2, gh, ghb = pl.pallas_call(
        finish,
        out_shape=(
            shape((1, 4), F32), shape((27, 4, 16), F32), shape((1, 16), F32), shape((432, 128), F32),
            shape((1, 128), F32), shape((4, 128), F32), shape((1, 4), F32),
        ),
        in_specs=[pl.BlockSpec(memory_space=pltpu.VMEM)] * 2,
        out_specs=[pl.BlockSpec(memory_space=pltpu.VMEM)] * 7,
    )(res, pred)
    gk1 = gk1.reshape(3, 3, 3, 4, 16).transpose(4, 3, 0, 1, 2)
    gk2 = gk2.reshape(3, 3, 3, 16, 128).transpose(4, 3, 0, 1, 2)
    return pred, gk1, gb1[0], gk2, gb2[0], gh, ghb[0]


def solution(mesh):
    in_specs = (P("dp", None, "space", None, None), P("dp", None), P(), P(), P(), P(), P(), P())
    out_specs = (P("dp", None), P(), P(), P(), P(), P(), P())
    return jax.shard_map(body, mesh=mesh, in_specs=in_specs, out_specs=out_specs, check_vma=False)
```

```python
import functools

import jax
import jax.numpy as jnp
from jax import lax
from jax.experimental import pallas as pl
from jax.experimental.pallas import tpu as pltpu
from jax.sharding import PartitionSpec as P

F32 = jnp.float32
BF16 = jnp.bfloat16
MESH = pl.DeviceIdType.MESH
NT = (((1,), (1,)), ((), ()))
TN = (((0,), (0,)), ((), ()))
EARLY = 448
ROWS = 512


def iota(shape, dim):
    return lax.broadcasted_iota(jnp.int32, shape, dim)


def dot(a, b, dims=(((1,), (0,)), ((), ())), precision=None):
    return lax.dot_general(a, b, dims, precision=precision, preferred_element_type=F32)


def to_column(row):
    n = row.shape[1]
    return jnp.sum(jnp.where(iota((n, n), 0) == iota((n, n), 1), row, 0.0), axis=1, keepdims=True)


def to_row(column):
    n = column.shape[0]
    return jnp.sum(jnp.where(iota((n, n), 0) == iota((n, n), 1), column, 0.0), axis=0, keepdims=True)


def shifted(block, dz):
    if dz == 1:
        return block
    lane = iota(block.shape, 1)
    if dz == 0:
        return jnp.where(lane == 0, 0.0, pltpu.roll(block, 1, 1))
    return jnp.where(lane == 127, 0.0, pltpu.roll(block, 127, 1))


def kernel(
    n, nd,
    vol, tgt, k1, b1, k2t, b2, hw, hb,
    res, pred_o,
    k1s, lo1, hi1, lo2, hi2, patch, patch3, w1, own1, pz, p2, mk, mo, zs, ga, gg, acc1,
    fbuf, buf, rsbuf, dpbuf,
    h_send, h_recv, f_send, f_recv, r_send, r_recv, d_send, d_recv, g_send, g_recv,
):
    me = lax.axis_index("space")
    md = lax.axis_index("dp")
    samples = nd
    cells_two = 2 * 8 * 128 * n
    shard = buf.shape[0] // n

    def peer(j):
        return lax.rem(me + j, n)

    def dpeer(j):
        return lax.rem(md + j, nd)

    barrier = pltpu.get_barrier_semaphore()
    for j in range(1, n):
        pl.semaphore_signal(barrier, inc=1, device_id={"space": peer(j)}, device_id_type=MESH)
    for j in range(1, nd):
        pl.semaphore_signal(barrier, inc=1, device_id={"dp": dpeer(j)}, device_id_type=MESH)

    def remote(src, dst, send, recv, axis, to):
        return pltpu.make_async_remote_copy(
            src_ref=src, dst_ref=dst, send_sem=send, recv_sem=recv,
            device_id={axis: to}, device_id_type=MESH,
        )

    split = (iota((256, 512), 0) == 2 * (iota((256, 512), 1) & 127) + (iota((256, 512), 1) >> 7) - 1)
    split = split.astype(F32).astype(BF16)

    def place(blocks, first):
        rows = jnp.concatenate([blk.reshape(64, 256) for blk in blocks], axis=0)
        parts = dot(rows, split).astype(BF16)
        for i in range(len(blocks)):
            for s in range(4):
                patch[s * 64:(s + 1) * 64, (first + i) * 128:(first + i + 1) * 128] = (
                    parts[i * 64:(i + 1) * 64, s * 128:(s + 1) * 128]
                )

    pl.semaphore_wait(barrier, n - 1 + nd - 1)

    first = [vol, vol, vol.at[:, 3:4], vol.at[:, 0:1]]
    into = [lo1, hi1, lo2, hi2]
    steps = [1, -1, 2, -2]
    halo = [
        remote(first[i], into[i], h_send.at[i], h_recv.at[i], "space", lax.rem(me + steps[i] + n, n))
        for i in range(4)
    ]
    has_to = [me < n - 1, me > 0, me < n - 2, me > 1]
    has_from = [me > 0, me < n - 1, me > 1, me < n - 2]
    for i in range(4):
        pl.when(has_to[i])(halo[i].start)
    for i in range(4):
        @pl.when(jnp.logical_not(has_from[i]))
        def _(i=i):
            into[i][...] = jnp.zeros_like(into[i])

    place([vol[:, x] for x in range(4)], 5)

    col = iota((12, 512), 1)
    tap = iota((12, 512), 0)
    pick = (((col & 63) >> 4) == (tap & 3)) & (((col & 255) >> 6) == (col >> 8) + (tap >> 2))
    for t in range(9):
        for dz in range(3):
            k1s[dz * 4:(dz + 1) * 4, t * 16:(t + 1) * 16] = k1[t * 3 + dz].astype(F32)
    spread = dot(k1s[0:12, 0:144].astype(BF16), pick.astype(F32).astype(BF16), TN)
    ycol = iota((16, 256), 1) & 15
    for dx in range(3):
        for p in range(2):
            e = [spread[(dx * 3 + dy) * 16:(dx * 3 + dy + 1) * 16, p * 256:(p + 1) * 256] for dy in range(3)]
            for q in range(2):
                for yh in range(8):
                    y = 2 * yh + q
                    block = jnp.where(
                        ycol == y - 1, e[0],
                        jnp.where(ycol == y, e[1], jnp.where(ycol == y + 1, e[2], 0.0)),
                    )
                    r = p * 256 + (q * 8 + yh) * 16
                    w1[r:r + 16, dx * 256:(dx + 1) * 256] = block.astype(BF16)
    bias1 = jnp.broadcast_to(to_column(b1[...]), (16, 128))
    bias1 = jnp.concatenate([bias1] * 8, axis=0)
    bias2 = jnp.broadcast_to(to_column(b2[...]), (128, 128))

    pz[:, 0:16, :] = jnp.zeros((3, 16, 768), BF16)
    pz[:, 144:160, :] = jnp.zeros((3, 16, 768), BF16)
    p2[432:448, :] = jnp.ones((16, 4096), BF16)
    own = ((iota((128, 512), 1) >= 128) & (iota((128, 512), 1) < 384)).astype(F32)
    for y in range(8):
        mo[128:256, y * 512:(y + 1) * 512] = own.astype(BF16)
    buf[EARLY:, :] = jnp.zeros((buf.shape[0] - EARLY, 128), F32)

    for i in range(4):
        pl.when(has_from[i])(halo[i].wait_recv)
    place([lo2[:, 0]] + [lo1[:, x] for x in range(4)], 0)
    place([hi1[:, x] for x in range(4)] + [hi2[:, 0]], 9)
    for dx in range(3):
        patch3[dx * 256:(dx + 1) * 256, :] = patch[:, dx * 128:dx * 128 + 1536]

    low_ok = jnp.where(me > 0, 1.0, 0.0).astype(F32)
    high_ok = jnp.where(me < n - 1, 1.0, 0.0).astype(F32)
    for xp in range(6):
        pre = dot(w1[...], patch3[:, xp * 256:(xp + 1) * 256])
        total = None
        for r in range(4):
            for x in range(2):
                part = pre[r * 128:(r + 1) * 128, x * 128:(x + 1) * 128] + bias1
                if 2 <= xp < 4:
                    c = (xp - 2) * 256 + x * 128
                    own1[r * 128:(r + 1) * 128, c:c + 128] = part
                part = jnp.where(part > 0, part, 0.3 * part)
                total = part if total is None else total + part
        total = total * 0.125
        if xp < 2:
            total = total * low_ok
        if xp > 3:
            total = total * high_ok
        for dz in range(3):
            pz[dz, 16:144, xp * 128:(xp + 1) * 128] = shifted(total, dz).astype(BF16)

    for dx in range(3):
        for dy in range(3):
            for dz in range(3):
                t = (dx * 3 + dy) * 3 + dz
                for y in range(8):
                    p2[t * 16:(t + 1) * 16, y * 512:(y + 1) * 512] = (
                        pz[dz, (y + dy) * 16:(y + dy + 1) * 16, dx * 128:dx * 128 + 512]
                    )

    fsum = jnp.zeros((128, 128), F32)
    for y in range(8):
        pre = dot(k2t[...], p2[0:432, y * 512:(y + 1) * 512], TN)
        for x in range(4):
            lanes = slice(y * 512 + x * 128, y * 512 + (x + 1) * 128)
            part = pre[:, x * 128:(x + 1) * 128] + bias2
            mask = jnp.where(part > 0, 1.0, 0.0)
            mk[:, lanes] = mask.astype(BF16)
            if 1 <= x < 3:
                fsum = fsum + jnp.where(part > 0, part, 0.3 * part)
                mo[0:128, lanes] = mask.astype(BF16)
            else:
                mo[0:128, lanes] = jnp.zeros((128, 128), BF16)

    frow = jnp.sum(fsum.T, axis=0, keepdims=True)
    fbuf[me] = jnp.broadcast_to(frow, (8, 128))
    feats = [
        remote(fbuf.at[me], fbuf.at[me], f_send.at[j], f_recv.at[me], "space", peer(j))
        for j in range(1, n)
    ]
    for copy in feats:
        copy.start()

    sums = dot(p2[...], mo[...], NT)

    def arrived(slots, sems, axis, source):
        remote(slots.at[source], slots.at[source], f_send.at[0], sems.at[source], axis, source).wait_recv()

    for j in range(1, n):
        arrived(fbuf, f_recv, "space", peer(j))
    total = fbuf[0]
    for s in range(1, n):
        total = total + fbuf[s]
    features = total[0:4] / cells_two
    head = hw[...]
    prediction = jnp.sum(head * features, axis=1, keepdims=True) + to_column(hb[...])
    grad_pred = 2.0 * (prediction - to_column(tgt[...])) / samples
    pred_o[...] = jnp.broadcast_to(prediction, (4, 128))
    scaled = jnp.sum(head * grad_pred, axis=0, keepdims=True) / cells_two
    plus = scaled.astype(BF16).astype(F32)
    minus = (0.3 * scaled).astype(BF16).astype(F32)
    leader = jnp.where(me == 0, 1.0, 0.0).astype(F32)

    buf[0:EARLY, :] = sums[:, 128:256] * minus + sums[:, 0:128] * (plus - minus)
    buf[496:500, :] = leader * (grad_pred * features)
    buf[504:508, :] = leader * jnp.broadcast_to(grad_pred, (4, 128))

    whole = EARLY // shard
    scatter = [
        remote(
            buf.at[pl.ds(pl.multiple_of(peer(j) * shard, 8), shard)], rsbuf.at[me],
            r_send.at[j], r_recv.at[me], "space", peer(j),
        )
        for j in range(1, n)
    ]
    for j in range(1, n):
        pl.when(peer(j) < whole)(scatter[j - 1].start)

    plus_c = jnp.broadcast_to(plus, (128, 128)).T
    minus_c = jnp.broadcast_to(minus, (128, 128)).T
    for y in range(8):
        parts = []
        for x in range(4):
            part = mk[:, y * 512 + x * 128:y * 512 + (x + 1) * 128].astype(F32)
            part = jnp.where(part > 0, plus_c, minus_c)
            if x == 0:
                part = part * low_ok
            if x == 3:
                part = part * high_ok
            parts.append(part.astype(BF16))
        zs[:, y * 512:(y + 1) * 512] = dot(k2t[...], jnp.concatenate(parts, axis=1))
    for y in range(8):
        for dz in range(3):
            total = None
            for dx in range(3):
                for dy in range(3):
                    ys = y + 1 - dy
                    if 0 <= ys < 8:
                        t = (dx * 3 + dy) * 3 + dz
                        c = ys * 512 + (2 - dx) * 128
                        part = zs[t * 16:(t + 1) * 16, c:c + 256]
                        total = part if total is None else total + part
            ga[dz, y * 16:(y + 1) * 16, :] = total
    bsum = jnp.zeros((16, 128), F32)
    for xp in range(2):
        lanes = slice(xp * 128, (xp + 1) * 128)
        g = shifted(ga[0, :, lanes], 2) + ga[1, :, lanes] + shifted(ga[2, :, lanes], 0)
        g = g * 0.125
        low = 0.3 * g
        for r in range(4):
            for x in range(2):
                c = xp * 256 + x * 128
                part = jnp.where(own1[r * 128:(r + 1) * 128, c:c + 128] > 0, g, low).astype(BF16)
                gg[r * 128:(r + 1) * 128, c:c + 128] = part
                part = part.astype(F32)
                for k in range(8):
                    bsum = bsum + part[k * 16:(k + 1) * 16]
    across = [
        remote(dpbuf.at[md], dpbuf.at[md], d_send.at[j], d_recv.at[md], "dp", dpeer(j))
        for j in range(1, nd)
    ]

    def combine():
        for j in range(1, n):
            arrived(rsbuf, r_recv, "space", peer(j))
        rsbuf[me] = buf[pl.ds(pl.multiple_of(me * shard, 8), shard), :]
        total = rsbuf[0]
        for s in range(1, n):
            total = total + rsbuf[s]
        dpbuf[md] = total
        for copy in across:
            copy.start()

    pl.when(me < whole)(combine)
    for dx in range(3):
        full = dot(gg[...], patch3[dx * 256:(dx + 1) * 256, 512:1024], NT)
        for p in range(2):
            accs = [jnp.zeros((16, 256), F32)] * 3
            for q in range(2):
                for yh in range(8):
                    y = 2 * yh + q
                    r = p * 256 + (q * 8 + yh) * 16
                    block = full[r:r + 16, :]
                    for dy in range(3):
                        accs[dy] = accs[dy] + jnp.where(ycol == y + dy - 1, block, 0.0)
            for dy in range(3):
                r = (dx * 3 + dy) * 16
                acc1[r:r + 16, p * 256:(p + 1) * 256] = accs[dy]
    col = iota((16, 512), 1)
    tap = iota((16, 512), 0)
    pick = (((col & 63) >> 4) == (tap & 3)) & (((col & 255) >> 6) == (col >> 8) + (tap >> 2)) & (tap < 12)
    first = dot(pick.astype(F32), acc1[...], NT, lax.Precision.HIGHEST)
    buf[448:464, :] = first[:, 0:128]
    buf[464:480, 0:16] = first[:, 128:144]
    buf[480:496, :] = jnp.broadcast_to(jnp.sum(bsum, axis=1, keepdims=True), (16, 128))
    for j in range(1, n):
        pl.when(peer(j) >= whole)(scatter[j - 1].start)

    pl.when(me >= whole)(combine)
    for j in range(1, nd):
        arrived(dpbuf, d_recv, "dp", dpeer(j))
    total = dpbuf[0]
    for s in range(1, nd):
        total = total + dpbuf[s]
    mine = pl.ds(pl.multiple_of(me * shard, 16), shard)
    res[mine, :] = total.astype(BF16)
    gather = [
        remote(res.at[mine], res.at[mine], g_send.at[j], g_recv.at[me], "space", peer(j))
        for j in range(1, n)
    ]
    for copy in gather:
        copy.start()
    for j in range(1, n):
        source = peer(j)
        part = res.at[pl.ds(pl.multiple_of(source * shard, 16), shard)]
        remote(part, part, f_send.at[0], g_recv.at[source], "space", source).wait_recv()

    for i in range(4):
        pl.when(has_to[i])(halo[i].wait_send)
    for copy in feats + scatter + across + gather:
        copy.wait_send()


def finish(res, pred, pred_o, gk1_o, gb1_o, gk2_o, gb2_o, gh_o, ghb_o):
    gk2_o[...] = res[0:432, :].astype(F32)
    rest = res[432:512, :].astype(F32)
    gb2_o[...] = rest[0:1]
    for t in range(9):
        r, c = (16, t * 16) if t < 8 else (32, 0)
        for dz in range(3):
            gk1_o[t * 3 + dz] = rest[r + dz * 4:r + (dz + 1) * 4, c:c + 16]
    gb1_o[...] = to_row(rest[48:64, 0:1])
    gh_o[...] = rest[64:68]
    ghb_o[...] = to_row(rest[72:76, 0:1])
    pred_o[...] = to_row(pred[:, 0:1])


def body(
    volumes, targets, first_kernel, first_bias, second_kernel, second_bias, head_weight, head_bias
):
    n = lax.axis_size("space")
    nd = lax.axis_size("dp")
    shard = -(-ROWS // (16 * n)) * 16
    k1 = first_kernel.transpose(2, 3, 4, 1, 0).reshape(27, 4, 16)
    k2t = second_kernel.transpose(2, 3, 4, 1, 0).reshape(432, 128)
    shape = jax.ShapeDtypeStruct
    sem = pltpu.SemaphoreType.DMA
    v = pltpu.VMEM
    res, pred = pl.pallas_call(
        functools.partial(kernel, n, nd),
        out_shape=(shape((n * shard, 128), BF16), shape((4, 128), F32)),
        in_specs=[pl.BlockSpec(memory_space=pltpu.VMEM)] * 8,
        out_specs=[pl.BlockSpec(memory_space=pltpu.VMEM)] * 2,
        scratch_shapes=[
            v((16, 256), F32),
            v((4, 4, 16, 256), BF16), v((4, 4, 16, 256), BF16),
            v((4, 1, 16, 256), BF16), v((4, 1, 16, 256), BF16),
            v((256, 1792), BF16), v((768, 1536), BF16), v((512, 768), BF16), v((512, 512), F32),
            v((3, 160, 768), BF16), v((448, 4096), BF16), v((128, 4096), BF16), v((256, 4096), BF16),
            v((432, 4096), F32), v((3, 128, 256), F32), v((512, 512), BF16), v((144, 512), F32),
            v((n, 8, 128), F32), v((n * shard, 128), F32), v((n, shard, 128), F32),
            v((nd, shard, 128), F32),
            sem((4,)), sem((4,)), sem((n,)), sem((n,)), sem((n,)), sem((n,)),
            sem((nd,)), sem((nd,)), sem((n,)), sem((n,)),
        ],
        compiler_params=pltpu.CompilerParams(
            collective_id=0, has_side_effects=True, vmem_limit_bytes=56 * 1024 * 1024
        ),
        cost_estimate=pl.CostEstimate(flops=5_000_000_000, bytes_accessed=2_000_000, transcendentals=0),
    )(
        volumes[0], targets, k1, first_bias[None], k2t, second_bias[None], head_weight, head_bias[None]
    )
    pred, gk1, gb1, gk2, gb2, gh, ghb = pl.pallas_call(
        finish,
        out_shape=(
            shape((1, 4), F32), shape((27, 4, 16), F32), shape((1, 16), F32), shape((432, 128), F32),
            shape((1, 128), F32), shape((4, 128), F32), shape((1, 4), F32),
        ),
        in_specs=[pl.BlockSpec(memory_space=pltpu.VMEM)] * 2,
        out_specs=[pl.BlockSpec(memory_space=pltpu.VMEM)] * 7,
    )(res, pred)
    gk1 = gk1.reshape(3, 3, 3, 4, 16).transpose(4, 3, 0, 1, 2)
    gk2 = gk2.reshape(3, 3, 3, 16, 128).transpose(4, 3, 0, 1, 2)
    return pred, gk1, gb1[0], gk2, gb2[0], gh, ghb[0]


def solution(mesh):
    in_specs = (P("dp", None, "space", None, None), P("dp", None), P(), P(), P(), P(), P(), P())
    out_specs = (P("dp", None), P(), P(), P(), P(), P(), P())
    return jax.shard_map(body, mesh=mesh, in_specs=in_specs, out_specs=out_specs, check_vma=False)
```
